128 devices in a mesh: row: 16 (over x_hi, y, core), col: 8 (over z, x_lo).
Axes of the slice: x: 4 (x_hi: 2, x_lo: 2; x = x_hi * 2 + x_lo), y: 4, z: 4, core: 2. Of those that a mesh axis runs over, the one named last changes fastest.
Arguments:
- blocks: bfloat16 [640, 24, 128, 128], P(('row', 'col')), may hold values from -0.8984375 to 0.8984375
- pattern: int32 [640, 24], P(('row', 'col')), may hold values from 0 to 639, as said below
- owner: int32 [15360, 1], P(('row', 'col')), may hold values from 0 to 127; in each aligned block of 120 rows (0 to 119, 120 to 239, ...) at most 2 rows name the same one
Outputs:
- owned_blocks: bfloat16 [32768, 128, 128], P(('row', 'col'))
- owned_ids: int32 [32768], P(('row', 'col'))
The draws below stay inside these ranges and needn't reach their ends.
Inputs may be any that keep to these rules, and one draw needn't show every extreme that they name: `pattern`: the 24 indices of a block row are distinct, and each names a block row held by the device of that row or by one of its eight neighbours on the periodic 16 by 8 device grid. Among the blocks of one device's block rows, at most 2 name the same owner; some owner receives exactly 2 from some device.
All inputs are finite; a program needn't handle non-finite values.
Results may differ from the reference program's by a relative error of at most 0.001.
Values may be sent and summed in bfloat16 or wider, within the bound.
No kernel may reach another device: no remote copies, remote signals or barrier semaphores. Data moves between devices by JAX's collectives and lax.ppermute only.
A program may use at most 192 MiB of HBM per device.

```python
import math
import jax
import jax.numpy as jnp
import numpy as np
from jax import lax

B = 128
S = 24
RD = 5
NB = 640
CAP = 2
N_ROW = 16
N_COL = 8


def draw_pattern(key, part):
    key = jax.random.fold_in(key, 11)
    choices_count = 9 * RD
    scores = jax.random.randint(key, (NB, choices_count), 0, 1 << 20)
    scores = scores * choices_count + jnp.arange(choices_count, dtype=jnp.int32)[None, :]
    order = jnp.argsort(scores, axis=1, stable=True)[:, :S].astype(jnp.int32)
    row_ids = jnp.arange(NB, dtype=jnp.int32)[:, None]
    device = row_ids // RD
    grid_row = device // N_COL
    grid_col = device % N_COL
    direction = order // RD
    local_row = order % RD
    step_row = direction // 3 - 1
    step_col = direction % 3 - 1
    other_row = (grid_row + step_row + N_ROW) % N_ROW
    other_col = (grid_col + step_col + N_COL) % N_COL
    return ((other_row * N_COL + other_col) * RD + local_row).astype(jnp.int32)


def levels(key, shape, split, smallest, top_value):
    def one(dim, blocks):
        heights = jax.random.uniform(jax.random.fold_in(jax.random.fold_in(key, 6), dim), (blocks,), jnp.float32, smallest / len(split), top_value / len(split))
        return jnp.repeat(jnp.exp(heights), shape[dim] // blocks).reshape((-1,) + (1,) * (len(shape) - dim - 1))

    level = one(*split[0])
    for cut in split[1:]:
        level = level * one(*cut)
    return level


def shared_out(stream_key, own, number, rows, amount, top, limit, slope):
    ranking = jax.random.permutation(stream_key, amount)
    packed, common = portions_of(amount, rows * top, limit, slope, True), portions_of(amount, rows * top, limit, slope, False)
    places = jnp.arange(amount)

    def named(tallies, turn):
        used = int((tallies > 0).sum())
        fixed = max(1, used // 4)
        moved = fixed + (places - fixed + turn * (used - fixed)) % max(1, amount - fixed)
        return jnp.zeros((amount,), jnp.int32).at[ranking[jnp.where(places < fixed, places, moved)]].set(jnp.asarray(tallies, jnp.int32))

    tallies = jnp.where(number % 4 == 0, named(packed, number // 4), named(common, number - number // 4 - 1))
    mixed = jax.random.permutation(jax.random.fold_in(own, 3), amount)
    source_of, taker = mixed[0:amount // 2 * 2:2], mixed[1:amount // 2 * 2:2]
    room = jnp.minimum(tallies[source_of] - 1, limit - tallies[taker]) // 2
    room = jnp.where((source_of == ranking[0]) | (taker == ranking[0]) | (tallies[taker] == 0), 0, jnp.maximum(room, 0))
    moved = jax.random.randint(jax.random.fold_in(own, 4), (amount // 2,), 0, 1 << 20) % (room + 1)
    tallies = tallies.at[source_of].add(-moved).at[taker].add(moved)
    items = jnp.searchsorted(jnp.cumsum(tallies), jnp.arange(rows * top), side="right").astype(jnp.int32)
    grid = items.reshape(top, rows).T
    grid = grid[jax.random.permutation(jax.random.fold_in(own, 1), rows)]
    turn = jax.random.randint(jax.random.fold_in(own, 2), (rows, 1), 0, top)
    return jnp.take_along_axis(grid, (jnp.arange(top)[None, :] + turn) % top, axis=1)


def portions_of(amount, total, limit, slope, full):
    weights = [(1 << 20) // math.isqrt(grade ** slope) + 1 for grade in range(1, amount + 1)]
    largest = limit if full else min(limit, max(-(-total // amount), total * weights[0] // sum(weights)))
    least = 1 if total - largest >= amount - 1 else 0
    counts, rest = [largest] + [least] * (amount - 1), total - largest - least * (amount - 1)
    while rest > 0:
        candidates = [i for i in range(1, amount) if counts[i] < largest] or [i for i in range(1, amount) if counts[i] < limit]
        whole, remaining = sum([weights[i] for i in candidates]), rest
        for i in candidates:
            addition = min(limit - counts[i], max(1, remaining * weights[i] // whole), rest)
            counts[i] = counts[i] + addition
            rest = rest - addition
    return np.array(counts)


def noise(stream_key, extent, spread, reach, cuts=(), held_as=jnp.bfloat16):
    array = spread * jax.random.normal(stream_key, extent, jnp.float32)
    if cuts:
        array = array * levels(stream_key, extent, cuts, -0.22, 0.18)
    return jnp.clip(array, -reach, reach).astype(held_as)


def setup_inputs(seed: int = 0) -> dict:
    streams_of = jax.random.split(jax.random.key(seed), 4)
    blocks = noise(streams_of[0], (NB, S, B, B), 0.15, 0.8984375, ((0, 128),))
    pattern = draw_pattern(jax.random.fold_in(streams_of[3], 71), 0)
    owner_keys = jax.random.split(jax.random.fold_in(streams_of[2], 1), (NB * S) // (RD * S))
    owner_turns = jax.random.permutation(jax.random.fold_in(streams_of[2], 3), (NB * S) // (RD * S))
    owner = jax.vmap(lambda own, number: shared_out(jax.random.fold_in(streams_of[2], 2), own, number, RD * S, N_ROW * N_COL, 1, CAP, 2))(owner_keys, owner_turns).reshape((NB * S, 1))
    return {"blocks": blocks, "pattern": pattern, "owner": owner}


def reference(blocks, pattern, owner):
    devices = N_ROW * N_COL
    flat_blocks = blocks.reshape(NB * S, B, B)

    def one_row(row_index):
        row_cols = pattern[row_index]
        inner_cols = pattern[row_cols]
        matches = inner_cols[:, None, :] == row_cols[None, :, None]
        found = jnp.any(matches, axis=2)
        where_slot = jnp.argmax(matches, axis=2).astype(jnp.int32)
        picked = flat_blocks[row_cols[:, None] * S + where_slot]
        picked = jnp.where(found[:, :, None, None], picked, jnp.zeros_like(picked))
        summed = jnp.einsum("axy,auyz->uxz", blocks[row_index].astype(jnp.float32), picked.astype(jnp.float32))
        return summed.astype(jnp.bfloat16)

    block_product = lax.map(one_row, jnp.arange(NB, dtype=jnp.int32))
    owners = owner.reshape(NB * S)
    source = (jnp.arange(NB * S, dtype=jnp.int32) // (RD * S)).astype(jnp.int32)
    one_hot = (owners[:, None] == jnp.arange(devices, dtype=jnp.int32)[None, :]).astype(jnp.int32)
    one_hot = one_hot.reshape(devices, RD * S, devices)
    running = jnp.cumsum(one_hot, axis=1) - 1
    rank = jnp.sum(running * one_hot, axis=2).reshape(NB * S).astype(jnp.int32)
    target = (owners * devices + source) * CAP + rank
    owned_blocks = jnp.zeros((devices * devices * CAP, B, B), jnp.bfloat16)
    owned_blocks = owned_blocks.at[target].set(block_product.reshape(NB * S, B, B))
    owned_ids = jnp.full((devices * devices * CAP,), -1, jnp.int32)
    owned_ids = owned_ids.at[target].set(jnp.arange(NB * S, dtype=jnp.int32))
    return owned_blocks, owned_ids
```

```python
import jax
import jax.numpy as jnp
from jax import lax
from jax.experimental import pallas as pl
from jax.experimental.pallas import tpu as pltpu
from jax.sharding import PartitionSpec as P

AXES = ("row", "col")
UNROLL = 24


def at_wrap(r, rows):
    half = rows // 2
    return r in (0, half - 1, half, rows - 1)


def permutations(rows, cols):
    def build(target):
        pairs = []
        for r in range(rows):
            for c in range(cols):
                tr, tc = target(r, c)
                pairs.append((r * cols + c, (tr % rows) * cols + tc % cols))
        return pairs

    def beside(r):
        return r + 1 if r % 2 else r - 1

    def along(c):
        return c + 2 if c % 2 == 0 else c - 2

    return {
        "pair": build(lambda r, c: (r, c ^ 1)),
        "skip": build(lambda r, c: (r, along(c))),
        "far": build(lambda r, c: (r, c - 1 if c % 2 == 0 else c + 1)),
        "core": build(lambda r, c: (r ^ 1, c)),
        "beside": build(lambda r, c: (beside(r), c)),
        "a": build(lambda r, c: (beside(r), c ^ 1) if at_wrap(r, rows) else (beside(r), c)),
        "b": build(lambda r, c: (r, c ^ 1) if at_wrap(r, rows) else (beside(r), c)),
        "c": build(lambda r, c: (r, along(c)) if at_wrap(r, rows) else (beside(r), c)),
    }


def pick(name, flag, a, b):
    def body(flag_ref, a_ref, b_ref, out_ref, sem):
        @pl.when(flag_ref[0] != 0)
        def _():
            copy = pltpu.make_async_copy(a_ref, out_ref, sem)
            copy.start()
            copy.wait()

        @pl.when(flag_ref[0] == 0)
        def _():
            copy = pltpu.make_async_copy(b_ref, out_ref, sem)
            copy.start()
            copy.wait()

    return pl.pallas_call(
        body,
        out_shape=jax.ShapeDtypeStruct(a.shape, a.dtype),
        in_specs=[pl.BlockSpec(memory_space=pltpu.SMEM)] + [pl.BlockSpec(memory_space=pl.ANY)] * 2,
        out_specs=pl.BlockSpec(memory_space=pltpu.VMEM),
        scratch_shapes=[pltpu.SemaphoreType.DMA],
        cost_estimate=pl.CostEstimate(flops=0, bytes_accessed=2 * a.size * 2, transcendentals=0),
        name=name,
    )(flag, a, b)


def add_entries(count_ref, list_ref, left_ref, pool, acc):
    def group(g, _):
        for q in range(UNROLL):
            code = list_ref[g * UNROLL + q]
            slot = code & 127
            block = (code >> 7) & 1023
            acc[slot] += jnp.dot(
                left_ref[code >> 17], pool[block], preferred_element_type=jnp.float32
            )
        return 0

    lax.fori_loop(0, (count_ref[0] + UNROLL - 1) // UNROLL, group, 0)


def load_pool(chunks, pool, sems):
    copies, start = [], 0
    for n, chunk in enumerate(chunks):
        size = chunk.shape[0]
        copies.append(pltpu.make_async_copy(chunk, pool.at[pl.ds(start, size)], sems.at[n]))
        start += size
    for copy in copies:
        copy.start()
    return copies


def accumulate(name, count, entries, left, chunks, acc):
    n = len(chunks)
    size = sum(chunk.shape[0] for chunk in chunks)
    order = left.shape[-1]
    slots = left.shape[0] + 8
    fresh = acc is None

    def body(*refs):
        count_ref, list_ref, left_ref = refs[:3]
        chunk_refs = refs[3 : 3 + n]
        out, total, pool, sems = refs[-4:]
        copies = load_pool(chunk_refs, pool, sems)
        if fresh:
            total[...] = jnp.zeros(total.shape, total.dtype)
        else:
            fetch = pltpu.make_async_copy(refs[3 + n], total, sems.at[n])
            fetch.start()
            copies.append(fetch)
        for copy in copies:
            copy.wait()
        add_entries(count_ref, list_ref, left_ref, pool, total)
        store = pltpu.make_async_copy(total, out, sems.at[n])
        store.start()
        store.wait()

    smem = pl.BlockSpec(memory_space=pltpu.SMEM)
    vmem = pl.BlockSpec(memory_space=pltpu.VMEM)
    anywhere = pl.BlockSpec(memory_space=pl.ANY)
    args = [count, entries, left, *chunks] + ([] if fresh else [acc])
    return pl.pallas_call(
        body,
        out_shape=jax.ShapeDtypeStruct((slots, order, order), jnp.float32),
        in_specs=[smem, smem, vmem] + [anywhere] * (n + (not fresh)),
        out_specs=anywhere,
        scratch_shapes=[
            pltpu.VMEM((slots, order, order), jnp.float32),
            pltpu.VMEM((size, order, order), jnp.bfloat16),
            pltpu.SemaphoreType.DMA((n + 1,)),
        ],
        input_output_aliases={} if fresh else {3 + n: 0},
        compiler_params=pltpu.CompilerParams(vmem_limit_bytes=36 << 20),
        cost_estimate=pl.CostEstimate(
            flops=size * 3 * order**3, bytes_accessed=size * order * order * 2 + 20 * 2**20, transcendentals=0
        ),
        name=name,
    )(*args)


def finish(name, count, entries, left, chunks, acc, inverse):
    n = len(chunks)
    size = sum(chunk.shape[0] for chunk in chunks)
    order = left.shape[-1]
    slots = inverse.shape[0]
    part = 16

    def body(*refs):
        count_ref, list_ref, inverse_ref, left_ref = refs[:4]
        chunk_refs = refs[4 : 4 + n]
        acc_ref, out, total, pool, stage, sems, out_sems = refs[4 + n :]
        copies = load_pool(chunk_refs, pool, sems)
        fetch = pltpu.make_async_copy(acc_ref, total, sems.at[n])
        fetch.start()
        for copy in copies:
            copy.wait()
        fetch.wait()
        add_entries(count_ref, list_ref, left_ref, pool, total)

        def piece(p):
            return pltpu.make_async_copy(
                stage.at[pl.ds(p * part, part)], out.at[pl.ds(p * part, part)], out_sems.at[p]
            )

        def fill(p, _):
            for q in range(part):
                s = p * part + q
                t = inverse_ref[s]
                value = total[jnp.maximum(t, 0)]
                stage[s] = jnp.where(t >= 0, value, 0.0).astype(jnp.bfloat16)
            piece(p).start()
            return 0

        lax.fori_loop(0, slots // part, fill, 0)

        def drain(p, _):
            piece(p).wait()
            return 0

        lax.fori_loop(0, slots // part, drain, 0)

    smem = pl.BlockSpec(memory_space=pltpu.SMEM)
    vmem = pl.BlockSpec(memory_space=pltpu.VMEM)
    anywhere = pl.BlockSpec(memory_space=pl.ANY)
    return pl.pallas_call(
        body,
        out_shape=jax.ShapeDtypeStruct((slots, order, order), jnp.bfloat16),
        in_specs=[smem] * 3 + [vmem] + [anywhere] * (n + 1),
        out_specs=anywhere,
        scratch_shapes=[
            pltpu.VMEM(acc.shape, jnp.float32),
            pltpu.VMEM((size, order, order), jnp.bfloat16),
            pltpu.VMEM((slots, order, order), jnp.bfloat16),
            pltpu.SemaphoreType.DMA((n + 1,)),
            pltpu.SemaphoreType.DMA((slots // part,)),
        ],
        compiler_params=pltpu.CompilerParams(vmem_limit_bytes=40 << 20),
        cost_estimate=pl.CostEstimate(
            flops=size * 3 * order**3, bytes_accessed=30 * 2**20, transcendentals=0
        ),
        name=name,
    )(count, entries, inverse, left, *chunks, acc)


def shards(blocks, pattern, owner):
    held, stored, order = blocks.shape[:3]
    rows, cols = lax.axis_size("row"), lax.axis_size("col")
    devices = rows * cols
    r, c = lax.axis_index("row"), lax.axis_index("col")
    here = r * cols + c
    perms = permutations(rows, cols)
    half = rows // 2
    wrap = (r == 0) | (r == half - 1) | (r == half) | (r == rows - 1)
    flag = wrap.astype(jnp.int32).reshape(1)
    items = held * stored

    token = [None]

    def send(x, which):
        if token[0] is not None:
            x, _ = lax.optimization_barrier((x, token[0]))
        return lax.ppermute(x, AXES, perms[which])

    def wait(x):
        if token[0] is None:
            token[0] = x
        else:
            token[0], _ = lax.optimization_barrier((x, token[0]))

    pattern_col = jnp.stack([pattern, lax.ppermute(pattern, AXES, perms["pair"]), lax.ppermute(pattern, AXES, perms["far"])])
    pattern_core = lax.ppermute(pattern_col, AXES, perms["core"])
    pattern_y = lax.ppermute(pattern_col, AXES, perms["beside"])
    pattern_a = jnp.where(wrap, pattern_y[1], pattern_y[0])
    pattern_b = jnp.where(wrap, pattern_y[0], pattern_y[1])
    patterns = jnp.stack([*pattern_col, *pattern_core, pattern_a, pattern_b, pattern_y[2]])
    pair = c ^ 1
    far = jnp.where(c % 2 == 0, c - 1 + cols, c + 1) % cols
    beside = jnp.where(r % 2 == 1, r + 1, r - 1 + rows) % rows
    holders = jnp.stack(
        [r * cols + c, r * cols + pair, r * cols + far]
        + [(r ^ 1) * cols + c, (r ^ 1) * cols + pair, (r ^ 1) * cols + far]
        + [
            beside * cols + jnp.where(wrap, pair, c),
            beside * cols + jnp.where(wrap, c, pair),
            beside * cols + far,
        ]
    )
    row_ids = holders[:, None] * held + jnp.arange(held, dtype=jnp.int32)[None, :]
    numbers = jnp.arange(stored, dtype=jnp.int32)
    same_row = row_ids[:, :, None, None] == pattern[None, None]
    left_of = jnp.sum(jnp.where(same_row, numbers, 0), axis=-1)
    has_row = jnp.any(same_row, axis=-1)
    same_col = patterns[:, :, :, None, None] == pattern[None, None, None]
    slot_of = jnp.sum(jnp.where(same_col, numbers, 0), axis=-1)
    has_col = jnp.any(same_col, axis=-1)
    row_base = jnp.arange(held, dtype=jnp.int32) * stored
    valid = has_row[:, :, None, :] & has_col
    codes = ((left_of + row_base)[:, :, None, :] << 17) | (slot_of + row_base)
    valid = valid.reshape(9, held, stored * held)
    codes = codes.reshape(9, held, stored * held)
    block_number = jnp.repeat(numbers, held)

    slot_index = {"O": 0, "X": 1, "Z": 2, "DO": 3, "DX": 4, "DZ": 5, "A": 6, "B": 7, "C": 8}

    def tables(keys):
        ok = jnp.stack([valid[slot_index[s], k] for s, k in keys]).reshape(-1)
        code = jnp.stack(
            [codes[slot_index[s], k] | ((block_number + n * stored) << 7) for n, (s, k) in enumerate(keys)]
        ).reshape(-1)
        total = ok.shape[0]
        length = -(-total // UNROLL) * UNROLL
        place = jnp.where(ok, jnp.cumsum(ok.astype(jnp.int32)) - 1, -1)
        hit = place[None, :] == jnp.arange(length, dtype=jnp.int32)[:, None]
        count = jnp.sum(ok.astype(jnp.int32)).reshape(1)
        listed = jnp.sum(jnp.where(hit, code[None, :], 0), axis=1)
        listed = jnp.where(jnp.arange(length) < count, listed, items)
        return count, listed

    owners = owner.reshape(items)
    number = jnp.arange(items, dtype=jnp.int32)
    earlier = (owners[:, None] == owners[None, :]) & (number[None, :] < number[:, None])
    rank = jnp.sum(earlier.astype(jnp.int32), axis=1)
    capacity = max(2, items // devices + 1)
    target = owners * capacity + rank
    landed = target[None, :] == jnp.arange(devices * capacity, dtype=jnp.int32)[:, None]
    inverse = jnp.sum(jnp.where(landed, number[None, :] + 1, 0), axis=1) - 1
    outgoing_ids = jnp.where(inverse >= 0, here * items + inverse, -1)
    arrived_ids = lax.all_to_all(
        outgoing_ids.reshape(devices, capacity), AXES, split_axis=0, concat_axis=0, tiled=True
    )

    left = blocks.reshape(items, order, order)
    got = {name: [None] * held for name in ("X", "Z", "DX", "DZ", "A", "B", "C")}
    for k in range(2):
        got["X"][k] = send(blocks[k], "pair")
        got["A"][k] = send(blocks[k], "a")
    got["DO"] = send(left, "core")

    def run(name, keys, acc):
        chunks, used, skip = [], [], 0
        for s, k in keys:
            if s in ("O", "DO"):
                if k == 0:
                    chunks.append(left if s == "O" else got["DO"])
            else:
                chunks.append(got[s][k])
        count, listed = tables(keys)
        return accumulate(name, count, listed, left, chunks, acc)

    every = range(held)
    acc = run("own", [("O", k) for k in every], None)
    for k in every:
        wait(got["A"][k])
        wait(got["X"][k])
        if k + 2 < held:
            got["X"][k + 2] = send(blocks[k + 2], "pair")
            got["A"][k + 2] = send(blocks[k + 2], "a")
        got["Z"][k] = send(got["X"][k], "skip")
        got["B"][k] = send(pick("pick_b", flag, got["A"][k], got["X"][k]), "b")
        got["DX"][k] = send(got["X"][k], "core")
        if k == 0:
            acc = run("core", [("DO", j) for j in every], acc)
        else:
            wait(got["Z"][k - 1])
            got["C"][k - 1] = send(pick("pick_c", flag, got["A"][k - 1], got["Z"][k - 1]), "c")
            got["DZ"][k - 1] = send(got["Z"][k - 1], "core")
        if k == 2:
            acc = run("first", [("X", 0), ("X", 1), ("A", 0), ("A", 1), ("DX", 0), ("DX", 1), ("Z", 0), ("B", 0)], acc)
        if k == 4:
            acc = run(
                "second",
                [("X", 2), ("X", 3), ("A", 2), ("A", 3), ("DX", 2), ("DX", 3), ("Z", 1), ("Z", 2)]
                + [("DZ", 0), ("DZ", 1), ("B", 1), ("B", 2), ("C", 0)],
                acc,
            )
    last = held - 1
    wait(got["Z"][last])
    got["C"][last] = send(pick("pick_c", flag, got["A"][last], got["Z"][last]), "c")
    got["DZ"][last] = send(got["Z"][last], "core")
    acc = run(
        "third",
        [("X", 4), ("A", 4), ("DX", 4), ("Z", 3), ("Z", 4), ("DZ", 2), ("DZ", 3), ("B", 3), ("C", 1), ("C", 2)],
        acc,
    )
    keys = [("B", 4), ("C", 3), ("C", 4), ("DZ", 4)]
    count, listed = tables(keys)
    outgoing = finish("finish", count, listed, left, [got[s][k] for s, k in keys], acc, inverse)
    arrived = lax.all_to_all(outgoing, AXES, split_axis=0, concat_axis=0, tiled=True)
    return arrived, arrived_ids.reshape(devices * capacity)


def solution(mesh):
    in_specs = (P(AXES, None, None, None), P(AXES, None), P(AXES, None))
    out_specs = (P(AXES, None, None), P(AXES))
    return jax.shard_map(shards, mesh=mesh, in_specs=in_specs, out_specs=out_specs, check_vma=False)
```

```python
import jax
import jax.numpy as jnp
from jax import lax
from jax.experimental import pallas as pl
from jax.experimental.pallas import tpu as pltpu
from jax.sharding import PartitionSpec as P

AXES = ("row", "col")
UNROLL = 24


def at_wrap(r, rows):
    half = rows // 2
    return r in (0, half - 1, half, rows - 1)


def permutations(rows, cols):
    def build(target):
        pairs = []
        for r in range(rows):
            for c in range(cols):
                reached = target(r, c)
                if reached is None:
                    continue
                tr, tc = reached
                pairs.append((r * cols + c, (tr % rows) * cols + tc % cols))
        return pairs

    def beside(r):
        return r + 1 if r % 2 else r - 1

    def along(c):
        return c + 2 if c % 2 == 0 else c - 2

    def only(wrapped, target):
        return build(lambda r, c: target(r, c) if at_wrap(r, rows) == wrapped else None)

    def other(c):
        return c - 1 if c % 2 == 0 else c + 1

    def back(c):
        return c - 2 if c % 2 == 0 else c + 2

    return {
        "pair": build(lambda r, c: (r, c ^ 1)),
        "along": build(lambda r, c: (r, along(c))),
        "far": build(lambda r, c: (r, other(c))),
        "core": build(lambda r, c: (r ^ 1, c)),
        "beside": build(lambda r, c: (beside(r), c)),
        "cross": build(lambda r, c: (beside(r), c ^ 1) if at_wrap(r, rows) else (beside(r), c)),
        "inner_beside": only(False, lambda r, c: (beside(r), c)),
        "wrap_pair": only(True, lambda r, c: (r, c ^ 1)),
        "wrap_back": only(True, lambda r, c: (r, back(c))),
        "wrap_cross": only(True, lambda r, c: (beside(r), c ^ 1)),
    }


def add_entries(count_ref, list_ref, left_ref, pool, acc):
    def group(g, _):
        for q in range(UNROLL):
            code = list_ref[g * UNROLL + q]
            slot = code & 127
            block = (code >> 7) & 1023
            acc[slot] += jnp.dot(
                left_ref[code >> 17], pool[block], preferred_element_type=jnp.float32
            )
        return 0

    lax.fori_loop(0, (count_ref[0] + UNROLL - 1) // UNROLL, group, 0)


def load_pool(flag_ref, refs, chunks, pool, sems):
    refs, copies, start = list(refs), [], 0
    for n, chunk in enumerate(chunks):
        size = chunk[-1].shape[0]
        into = pool.at[pl.ds(start, size)]
        if len(chunk) == 1:
            copies.append(pltpu.make_async_copy(refs.pop(0), into, sems.at[n]))
            copies[-1].start()
        else:
            at_cut = pltpu.make_async_copy(refs.pop(0).at[pl.ds(chunk[1], size)], into, sems.at[n])
            elsewhere = pltpu.make_async_copy(refs.pop(0), into, sems.at[n])
            pl.when(flag_ref[0] != 0)(at_cut.start)
            pl.when(flag_ref[0] == 0)(elsewhere.start)
            copies.append(elsewhere)
        start += size
    return copies


def arrays_of(chunks):
    return [one for chunk in chunks for one in chunk if not isinstance(one, int)]


def accumulate(name, flag, count, entries, left, chunks, acc):
    arrays = arrays_of(chunks)
    n, size = len(arrays), sum(chunk[-1].shape[0] for chunk in chunks)
    order = left.shape[-1]
    slots = left.shape[0] + 8
    fresh = acc is None

    def body(*refs):
        flag_ref, count_ref, list_ref, left_hbm = refs[:4]
        out, total, left_ref, pool, sems = refs[-5:]
        fetch_left = pltpu.make_async_copy(left_hbm, left_ref, sems.at[n + 1])
        fetch_left.start()
        copies = load_pool(flag_ref, refs[4 : 4 + n], chunks, pool, sems)
        if fresh:
            total[...] = jnp.zeros(total.shape, total.dtype)
        else:
            fetch = pltpu.make_async_copy(refs[4 + n], total, sems.at[n])
            fetch.start()
            copies.append(fetch)
        for copy in [fetch_left, *copies]:
            copy.wait()
        add_entries(count_ref, list_ref, left_ref, pool, total)
        store = pltpu.make_async_copy(total, out, sems.at[n])
        store.start()
        store.wait()

    smem = pl.BlockSpec(memory_space=pltpu.SMEM)
    anywhere = pl.BlockSpec(memory_space=pl.ANY)
    args = [flag, count, entries, left, *arrays] + ([] if fresh else [acc])
    return pl.pallas_call(
        body,
        out_shape=jax.ShapeDtypeStruct((slots, order, order), jnp.float32),
        in_specs=[smem] * 3 + [anywhere] * (1 + n + (not fresh)),
        out_specs=anywhere,
        scratch_shapes=[
            pltpu.VMEM((slots, order, order), jnp.float32),
            pltpu.VMEM(left.shape, jnp.bfloat16),
            pltpu.VMEM((size, order, order), jnp.bfloat16),
            pltpu.SemaphoreType.DMA((n + 2,)),
        ],
        input_output_aliases={} if fresh else {4 + n: 0},
        compiler_params=pltpu.CompilerParams(vmem_limit_bytes=36 << 20),
        cost_estimate=pl.CostEstimate(flops=8 << 30, bytes_accessed=32 << 20, transcendentals=0),
        name=name,
    )(*args)


def finish(name, flag, count, entries, left, chunks, acc, inverse):
    arrays = arrays_of(chunks)
    n, size = len(arrays), sum(chunk[-1].shape[0] for chunk in chunks)
    order = left.shape[-1]
    slots = inverse.shape[0]
    part = 16

    def body(*refs):
        flag_ref, count_ref, list_ref, inverse_ref, left_hbm = refs[:5]
        acc_ref, out, total, left_ref, pool, stage, sems, out_sems = refs[5 + n :]
        fetch_left = pltpu.make_async_copy(left_hbm, left_ref, sems.at[n + 1])
        fetch_left.start()
        copies = load_pool(flag_ref, refs[5 : 5 + n], chunks, pool, sems)
        fetch = pltpu.make_async_copy(acc_ref, total, sems.at[n])
        fetch.start()
        for copy in [fetch_left, *copies, fetch]:
            copy.wait()
        add_entries(count_ref, list_ref, left_ref, pool, total)

        def piece(p):
            return pltpu.make_async_copy(
                stage.at[pl.ds(p * part, part)], out.at[pl.ds(p * part, part)], out_sems.at[p]
            )

        def fill(p, _):
            for q in range(part):
                s = p * part + q
                t = inverse_ref[s]
                value = total[jnp.maximum(t, 0)]
                stage[s] = jnp.where(t >= 0, value, 0.0).astype(jnp.bfloat16)
            piece(p).start()
            return 0

        lax.fori_loop(0, slots // part, fill, 0)

        def drain(p, _):
            piece(p).wait()
            return 0

        lax.fori_loop(0, slots // part, drain, 0)

    smem = pl.BlockSpec(memory_space=pltpu.SMEM)
    anywhere = pl.BlockSpec(memory_space=pl.ANY)
    return pl.pallas_call(
        body,
        out_shape=jax.ShapeDtypeStruct((slots, order, order), jnp.bfloat16),
        in_specs=[smem] * 4 + [anywhere] * (n + 2),
        out_specs=anywhere,
        scratch_shapes=[
            pltpu.VMEM(acc.shape, jnp.float32),
            pltpu.VMEM(left.shape, jnp.bfloat16),
            pltpu.VMEM((size, order, order), jnp.bfloat16),
            pltpu.VMEM((slots, order, order), jnp.bfloat16),
            pltpu.SemaphoreType.DMA((n + 2,)),
            pltpu.SemaphoreType.DMA((slots // part,)),
        ],
        compiler_params=pltpu.CompilerParams(vmem_limit_bytes=40 << 20),
        cost_estimate=pl.CostEstimate(flops=0, bytes_accessed=1 << 18, transcendentals=0),
        name=name,
    )(flag, count, entries, inverse, left, *arrays, acc)


def shards(blocks, pattern, owner):
    held, stored, order = blocks.shape[:3]
    rows, cols = lax.axis_size("row"), lax.axis_size("col")
    devices = rows * cols
    r, c = lax.axis_index("row"), lax.axis_index("col")
    here = r * cols + c
    perms = permutations(rows, cols)
    half = rows // 2
    wrap = (r == 0) | (r == half - 1) | (r == half) | (r == rows - 1)
    items = held * stored
    left = blocks.reshape(items, order, order)

    flag = [wrap.astype(jnp.int32).reshape(1)]
    got = {}

    def after(x):
        x, flag[0] = lax.optimization_barrier((x, flag[0]))
        return x

    def wait(*keys):
        for key in keys:
            got[key] = after(got[key])

    def send(x, which):
        return lax.ppermute(after(x), AXES, perms[which])

    pair = c ^ 1
    far = jnp.where(c % 2 == 0, c - 1 + cols, c + 1) % cols
    beside = jnp.where(r % 2 == 1, r + 1, r - 1 + rows) % rows
    holders = {
        "O": here,
        "X": r * cols + pair,
        "Z": r * cols + far,
        "DO": (r ^ 1) * cols + c,
        "DX": (r ^ 1) * cols + pair,
        "DZ": (r ^ 1) * cols + far,
        "A": beside * cols + jnp.where(wrap, pair, c),
        "B": beside * cols + jnp.where(wrap, c, pair),
        "C": beside * cols + far,
    }
    numbers = jnp.arange(stored, dtype=jnp.int32)
    own_slots = jnp.arange(items, dtype=jnp.int32).reshape(held, stored)

    def codes_of(patterns, ids, first):
        into = jnp.max(jnp.where(ids[:, None, None] == pattern[None], own_slots[None], -1), axis=-1)
        to = jnp.max(jnp.where(patterns[:, :, None, None] == pattern[None, None], own_slots[None, None], -1), axis=-1)
        into = into[:, None, :]
        block = (first[:, None] + numbers[None, :])[:, :, None]
        code = (into << 17) | (block << 7) | to
        return jnp.where((into >= 0) & (to >= 0), code, -1).reshape(patterns.shape[0], items)

    def listing(codes):
        codes = codes.reshape(-1)
        total = codes.shape[0]
        length = -(-total // UNROLL) * UNROLL
        ok = codes >= 0
        place = jnp.where(ok, jnp.cumsum(ok.astype(jnp.int32)) - 1, -1)
        count = jnp.sum(ok.astype(jnp.int32)).reshape(1)
        order_of = jnp.arange(length, dtype=jnp.int32)
        listed = jnp.sum(jnp.where(place[None, :] == order_of[:, None], codes[None, :], 0), axis=1)
        return count, jnp.where(order_of < count, listed, items)

    cuts = [(0, 3), (3, 5)]
    whole = (0, held)

    def rows_of(key):
        slot, p = key
        lo, hi = whole if p is None else cuts[p]
        return [(slot, k) for k in range(lo, hi)]

    calls = {
        "core": [("DO", None), ("A", None)],
        "first": [("X", 0), ("X", 1), ("Z", 0), ("DX", 0), ("DX", 1), ("DZ", 0)],
        "second": [("B", 0), ("B", 1), ("Z", 1), ("C", 0)],
        "last": [("C", 1), ("DZ", 1)],
    }

    def chunk_of(key):
        slot, p = key
        if slot in ("B", "C"):
            return (got["V" if slot == "B" else "F"], cuts[p][0] * stored, got[key])
        return (got[key],)

    x0 = left[cuts[0][0] * stored : cuts[0][1] * stored]
    got["DO", None] = send(left, "core")
    got["A", None] = send(left, "cross")
    got["X", 0] = send(x0, "pair")
    got["p2"] = send(pattern, "far")
    got["p1"] = send(pattern, "pair")
    wait("p1", "p2", ("DO", None))
    columns = jnp.stack([pattern, got["p1"], got["p2"]])
    got["W"] = send(left, "wrap_back")
    got["p3"] = send(columns, "core")
    got["p4"] = send(columns, "beside")
    got["x1"] = after(left)[cuts[1][0] * stored : cuts[1][1] * stored]
    own_codes = codes_of(after(pattern), here * held + jnp.arange(held), jnp.arange(held) * stored)
    got["own"] = listing(own_codes)
    wait("own")
    got["acc"] = accumulate("own", flag[0], *got["own"], left, [(left,)], None)
    owners = after(owner).reshape(items)
    number = jnp.arange(items, dtype=jnp.int32)
    earlier = (owners[:, None] == owners[None, :]) & (number[None, :] < number[:, None])
    rank = jnp.sum(earlier.astype(jnp.int32), axis=1)
    capacity = max(2, items // devices + 1)
    target = owners * capacity + rank
    landed = target[None, :] == jnp.arange(devices * capacity, dtype=jnp.int32)[:, None]
    got["inverse"] = jnp.sum(jnp.where(landed, number[None, :] + 1, 0), axis=1) - 1
    outgoing_ids = jnp.where(got["inverse"] >= 0, here * items + got["inverse"], -1)
    got["ids"] = lax.all_to_all(
        after(outgoing_ids).reshape(devices, capacity), AXES, split_axis=0, concat_axis=0, tiled=True
    )
    wait("acc", "W", ("A", None), "x1", "inverse", "p3", "p4")
    lists = {}
    core, near = got["p3"], got["p4"]
    patterns = {
        "O": pattern,
        "X": got["p1"],
        "Z": got["p2"],
        "DO": core[0],
        "DX": core[1],
        "DZ": core[2],
        "A": jnp.where(wrap, near[1], near[0]),
        "B": jnp.where(wrap, near[0], near[1]),
        "C": near[2],
    }
    pats, ids, first, bounds = [], [], [], [0]
    for names in calls.values():
        block = 0
        for key in names:
            for s, k in rows_of(key):
                pats.append(patterns[s][k : k + 1])
                ids.append(holders[s] * held + k)
                first.append(block)
                block += stored
        bounds.append(len(first))
    codes = codes_of(after(jnp.concatenate(pats)), jnp.stack(ids), jnp.asarray(first, jnp.int32))
    for name, lo, hi in zip(calls, bounds[:-1], bounds[1:]):
        lists[name] = listing(codes[lo:hi])

    for name in calls:
        lists[name] = tuple(after(x) for x in lists[name])
    wait(("X", 0))


    def run(name):
        chunks = [chunk_of(key) for key in calls[name]]
        got["acc"] = accumulate(name, flag[0], *lists[name], left, chunks, got["acc"])

    got["DX", 0] = send(got["X", 0], "core")
    got["F"] = send(got["W"], "wrap_cross")
    got["B", 0] = send(got["X", 0], "inner_beside")
    got["X", 1] = send(got["x1"], "pair")
    got["Z", 0] = send(got["X", 0], "along")
    run("core")
    wait("acc", ("Z", 0), ("X", 1), ("B", 0), "F", ("DX", 0))
    got["DX", 1] = send(got["X", 1], "core")
    got["B", 1] = send(got["X", 1], "inner_beside")
    got["V"] = send(got["A", None], "wrap_pair")
    got["C", 0] = send(got["Z", 0], "inner_beside")
    got["Z", 1] = send(got["X", 1], "along")
    wait(("DX", 1))
    got["DZ", 0] = send(got["Z", 0], "core")
    wait(("DZ", 0))
    run("first")
    wait("acc", "V", ("Z", 1), ("C", 0), ("B", 1), "ids")
    got["DZ", 1] = send(got["Z", 1], "core")
    got["C", 1] = send(got["Z", 1], "inner_beside")
    run("second")
    wait("acc", ("C", 1), ("DZ", 1))
    outgoing = finish(
        "last", flag[0], *lists["last"], left, [chunk_of(key) for key in calls["last"]], got["acc"], got["inverse"]
    )
    arrived_ids = got["ids"].reshape(devices * capacity)
    outgoing, arrived_ids = lax.optimization_barrier((outgoing, arrived_ids))
    arrived = lax.all_to_all(outgoing.reshape(-1, order), AXES, split_axis=0, concat_axis=0, tiled=True)
    arrived = arrived.reshape(outgoing.shape)
    return arrived, arrived_ids


def solution(mesh):
    in_specs = (P(AXES, None, None, None), P(AXES, None), P(AXES, None))
    out_specs = (P(AXES, None, None), P(AXES))
    return jax.shard_map(shards, mesh=mesh, in_specs=in_specs, out_specs=out_specs, check_vma=False)
```

```python
import jax
import jax.numpy as jnp
from jax import lax
from jax.experimental import pallas as pl
from jax.experimental.pallas import tpu as pltpu
from jax.sharding import PartitionSpec as P

AXES = ("row", "col")
UNROLL = 24


def at_wrap(r, rows):
    half = rows // 2
    return r in (0, half - 1, half, rows - 1)


def permutations(rows, cols):
    def build(target):
        pairs = []
        for r in range(rows):
            for c in range(cols):
                reached = target(r, c)
                if reached is None:
                    continue
                tr, tc = reached
                pairs.append((r * cols + c, (tr % rows) * cols + tc % cols))
        return pairs

    def beside(r):
        return r + 1 if r % 2 else r - 1

    def along(c):
        return c + 2 if c % 2 == 0 else c - 2

    def only(wrapped, target):
        return build(lambda r, c: target(r, c) if at_wrap(r, rows) == wrapped else None)

    def other(c):
        return c - 1 if c % 2 == 0 else c + 1

    def back(c):
        return c - 2 if c % 2 == 0 else c + 2

    return {
        "pair": build(lambda r, c: (r, c ^ 1)),
        "along": build(lambda r, c: (r, along(c))),
        "far": build(lambda r, c: (r, other(c))),
        "core": build(lambda r, c: (r ^ 1, c)),
        "beside": build(lambda r, c: (beside(r), c)),
        "cross": build(lambda r, c: (beside(r), c ^ 1) if at_wrap(r, rows) else (beside(r), c)),
        "inner_beside": only(False, lambda r, c: (beside(r), c)),
        "wrap_pair": only(True, lambda r, c: (r, c ^ 1)),
        "wrap_back": only(True, lambda r, c: (r, back(c))),
        "wrap_cross": only(True, lambda r, c: (beside(r), c ^ 1)),
    }


def add_entries(count_ref, list_ref, left_ref, pool, acc):
    def group(g, _):
        for q in range(UNROLL):
            code = list_ref[g * UNROLL + q]
            slot = code & 127
            block = (code >> 7) & 1023
            acc[slot] += jnp.dot(
                left_ref[code >> 17], pool[block], preferred_element_type=jnp.float32
            )
        return 0

    lax.fori_loop(0, (count_ref[0] + UNROLL - 1) // UNROLL, group, 0)


def load_pool(flag_ref, refs, chunks, pool, sems):
    refs, copies, start = list(refs), [], 0
    for n, chunk in enumerate(chunks):
        size = chunk[-1].shape[0]
        into = pool.at[pl.ds(start, size)]
        if len(chunk) == 1:
            copies.append(pltpu.make_async_copy(refs.pop(0), into, sems.at[n]))
            copies[-1].start()
        else:
            at_cut = pltpu.make_async_copy(refs.pop(0).at[pl.ds(chunk[1], size)], into, sems.at[n])
            elsewhere = pltpu.make_async_copy(refs.pop(0), into, sems.at[n])
            pl.when(flag_ref[0] != 0)(at_cut.start)
            pl.when(flag_ref[0] == 0)(elsewhere.start)
            copies.append(elsewhere)
        start += size
    return copies


def arrays_of(chunks):
    return [one for chunk in chunks for one in chunk if not isinstance(one, int)]


def accumulate(name, flag, count, entries, left, chunks, acc):
    arrays = arrays_of(chunks)
    n, size = len(arrays), sum(chunk[-1].shape[0] for chunk in chunks)
    order = left.shape[-1]
    slots = left.shape[0] + 8
    fresh = acc is None

    def body(*refs):
        flag_ref, count_ref, list_ref, left_hbm = refs[:4]
        out, total, left_ref, pool, sems = refs[-5:]
        fetch_left = pltpu.make_async_copy(left_hbm, left_ref, sems.at[n + 1])
        fetch_left.start()
        copies = load_pool(flag_ref, refs[4 : 4 + n], chunks, pool, sems)
        if fresh:
            total[...] = jnp.zeros(total.shape, total.dtype)
        else:
            fetch = pltpu.make_async_copy(refs[4 + n], total, sems.at[n])
            fetch.start()
            copies.append(fetch)
        for copy in [fetch_left, *copies]:
            copy.wait()
        add_entries(count_ref, list_ref, left_ref, pool, total)
        store = pltpu.make_async_copy(total, out, sems.at[n])
        store.start()
        store.wait()

    smem = pl.BlockSpec(memory_space=pltpu.SMEM)
    anywhere = pl.BlockSpec(memory_space=pl.ANY)
    args = [flag, count, entries, left, *arrays] + ([] if fresh else [acc])
    return pl.pallas_call(
        body,
        out_shape=jax.ShapeDtypeStruct((slots, order, order), jnp.float32),
        in_specs=[smem] * 3 + [anywhere] * (1 + n + (not fresh)),
        out_specs=anywhere,
        scratch_shapes=[
            pltpu.VMEM((slots, order, order), jnp.float32),
            pltpu.VMEM(left.shape, jnp.bfloat16),
            pltpu.VMEM((size, order, order), jnp.bfloat16),
            pltpu.SemaphoreType.DMA((n + 2,)),
        ],
        input_output_aliases={} if fresh else {4 + n: 0},
        compiler_params=pltpu.CompilerParams(vmem_limit_bytes=36 << 20),
        cost_estimate=pl.CostEstimate(flops=8 << 30, bytes_accessed=32 << 20, transcendentals=0),
        name=name,
    )(*args)


def finish(name, flag, count, entries, left, chunks, acc, inverse):
    arrays = arrays_of(chunks)
    n, size = len(arrays), sum(chunk[-1].shape[0] for chunk in chunks)
    order = left.shape[-1]
    slots = inverse.shape[0]
    part = 16

    def body(*refs):
        flag_ref, count_ref, list_ref, inverse_ref, left_hbm = refs[:5]
        acc_ref, out, total, left_ref, pool, stage, sems, out_sems = refs[5 + n :]
        fetch_left = pltpu.make_async_copy(left_hbm, left_ref, sems.at[n + 1])
        fetch_left.start()
        copies = load_pool(flag_ref, refs[5 : 5 + n], chunks, pool, sems)
        fetch = pltpu.make_async_copy(acc_ref, total, sems.at[n])
        fetch.start()
        for copy in [fetch_left, *copies, fetch]:
            copy.wait()
        add_entries(count_ref, list_ref, left_ref, pool, total)

        def piece(p):
            return pltpu.make_async_copy(
                stage.at[pl.ds(p * part, part)], out.at[pl.ds(p * part, part)], out_sems.at[p]
            )

        def fill(p, _):
            for q in range(part):
                s = p * part + q
                t = inverse_ref[s]
                value = total[jnp.maximum(t, 0)]
                stage[s] = jnp.where(t >= 0, value, 0.0).astype(jnp.bfloat16)
            piece(p).start()
            return 0

        lax.fori_loop(0, slots // part, fill, 0)

        def drain(p, _):
            piece(p).wait()
            return 0

        lax.fori_loop(0, slots // part, drain, 0)

    smem = pl.BlockSpec(memory_space=pltpu.SMEM)
    anywhere = pl.BlockSpec(memory_space=pl.ANY)
    return pl.pallas_call(
        body,
        out_shape=jax.ShapeDtypeStruct((slots, order, order), jnp.bfloat16),
        in_specs=[smem] * 4 + [anywhere] * (n + 2),
        out_specs=anywhere,
        scratch_shapes=[
            pltpu.VMEM(acc.shape, jnp.float32),
            pltpu.VMEM(left.shape, jnp.bfloat16),
            pltpu.VMEM((size, order, order), jnp.bfloat16),
            pltpu.VMEM((slots, order, order), jnp.bfloat16),
            pltpu.SemaphoreType.DMA((n + 2,)),
            pltpu.SemaphoreType.DMA((slots // part,)),
        ],
        compiler_params=pltpu.CompilerParams(vmem_limit_bytes=40 << 20),
        cost_estimate=pl.CostEstimate(flops=0, bytes_accessed=1 << 18, transcendentals=0),
        name=name,
    )(flag, count, entries, inverse, left, *arrays, acc)


def shards(blocks, pattern, owner):
    held, stored, order = blocks.shape[:3]
    rows, cols = lax.axis_size("row"), lax.axis_size("col")
    devices = rows * cols
    r, c = lax.axis_index("row"), lax.axis_index("col")
    here = r * cols + c
    perms = permutations(rows, cols)
    half = rows // 2
    wrap = (r == 0) | (r == half - 1) | (r == half) | (r == rows - 1)
    items = held * stored
    left = blocks.reshape(items, order, order)

    flag = [wrap.astype(jnp.int32).reshape(1)]
    got = {}

    def after(x):
        x, flag[0] = lax.optimization_barrier((x, flag[0]))
        return x

    def wait(*keys):
        for key in keys:
            got[key] = after(got[key])

    def send(x, which):
        return lax.ppermute(after(x), AXES, perms[which])

    pair = c ^ 1
    far = jnp.where(c % 2 == 0, c - 1 + cols, c + 1) % cols
    beside = jnp.where(r % 2 == 1, r + 1, r - 1 + rows) % rows
    holders = {
        "O": here,
        "X": r * cols + pair,
        "Z": r * cols + far,
        "DO": (r ^ 1) * cols + c,
        "DX": (r ^ 1) * cols + pair,
        "DZ": (r ^ 1) * cols + far,
        "A": beside * cols + jnp.where(wrap, pair, c),
        "B": beside * cols + jnp.where(wrap, c, pair),
        "C": beside * cols + far,
    }
    numbers = jnp.arange(stored, dtype=jnp.int32)
    own_slots = jnp.arange(items, dtype=jnp.int32).reshape(held, stored)

    def codes_of(patterns, ids, first):
        into = jnp.max(jnp.where(ids[:, None, None] == pattern[None], own_slots[None], -1), axis=-1)
        to = jnp.max(jnp.where(patterns[:, :, None, None] == pattern[None, None], own_slots[None, None], -1), axis=-1)
        into = into[:, None, :]
        block = (first[:, None] + numbers[None, :])[:, :, None]
        code = (into << 17) | (block << 7) | to
        return jnp.where((into >= 0) & (to >= 0), code, -1).reshape(patterns.shape[0], items)

    def listing(codes):
        codes = codes.reshape(-1)
        total = codes.shape[0]
        length = -(-total // UNROLL) * UNROLL
        ok = codes >= 0
        place = jnp.where(ok, jnp.cumsum(ok.astype(jnp.int32)) - 1, -1)
        count = jnp.sum(ok.astype(jnp.int32)).reshape(1)
        order_of = jnp.arange(length, dtype=jnp.int32)
        listed = jnp.sum(jnp.where(place[None, :] == order_of[:, None], codes[None, :], 0), axis=1)
        return count, jnp.where(order_of < count, listed, items)

    cuts = [(0, 3), (3, 5)]
    whole = (0, held)

    def rows_of(key):
        slot, p = key
        lo, hi = whole if p is None else cuts[p]
        return [(slot, k) for k in range(lo, hi)]

    calls = {
        "core": [("DO", None), ("A", None)],
        "first": [("X", 0), ("X", 1), ("Z", 0), ("DX", 0)],
        "second": [("B", 0), ("B", 1), ("Z", 1), ("C", 0), ("DZ", 0)],
        "last": [("C", 1), ("DZ", 1), ("DX", 1)],
    }

    def chunk_of(key):
        slot, p = key
        if slot in ("B", "C"):
            return (got["V" if slot == "B" else "F"], cuts[p][0] * stored, got[key])
        return (got[key],)

    x0 = left[cuts[0][0] * stored : cuts[0][1] * stored]
    got["DO", None] = send(left, "core")
    got["A", None] = send(left, "cross")
    got["X", 0] = send(x0, "pair")
    got["p2"] = send(pattern, "far")
    got["p1"] = send(pattern, "pair")
    wait("p1", "p2", ("DO", None))
    columns = jnp.stack([pattern, got["p1"], got["p2"]])
    got["W"] = send(left, "wrap_back")
    got["p3"] = send(columns, "core")
    got["p4"] = send(columns, "beside")
    got["x1"] = after(left)[cuts[1][0] * stored : cuts[1][1] * stored]
    own_codes = codes_of(after(pattern), here * held + jnp.arange(held), jnp.arange(held) * stored)
    got["own"] = listing(own_codes)
    wait("own")
    got["acc"] = accumulate("own", flag[0], *got["own"], left, [(left,)], None)
    owners = after(owner).reshape(items)
    number = jnp.arange(items, dtype=jnp.int32)
    earlier = (owners[:, None] == owners[None, :]) & (number[None, :] < number[:, None])
    rank = jnp.sum(earlier.astype(jnp.int32), axis=1)
    capacity = max(2, items // devices + 1)
    target = owners * capacity + rank
    landed = target[None, :] == jnp.arange(devices * capacity, dtype=jnp.int32)[:, None]
    got["inverse"] = jnp.sum(jnp.where(landed, number[None, :] + 1, 0), axis=1) - 1
    outgoing_ids = jnp.where(got["inverse"] >= 0, here * items + got["inverse"], -1)
    got["ids"] = lax.all_to_all(
        after(outgoing_ids).reshape(devices, capacity), AXES, split_axis=0, concat_axis=0, tiled=True
    )
    wait("acc", "W", ("A", None), "x1", "inverse", "p3", "p4")
    lists = {}
    core, near = got["p3"], got["p4"]
    patterns = {
        "O": pattern,
        "X": got["p1"],
        "Z": got["p2"],
        "DO": core[0],
        "DX": core[1],
        "DZ": core[2],
        "A": jnp.where(wrap, near[1], near[0]),
        "B": jnp.where(wrap, near[0], near[1]),
        "C": near[2],
    }
    pats, ids, first, bounds = [], [], [], [0]
    for names in calls.values():
        block = 0
        for key in names:
            for s, k in rows_of(key):
                pats.append(patterns[s][k : k + 1])
                ids.append(holders[s] * held + k)
                first.append(block)
                block += stored
        bounds.append(len(first))
    codes = codes_of(after(jnp.concatenate(pats)), jnp.stack(ids), jnp.asarray(first, jnp.int32))
    ranges = dict(zip(calls, zip(bounds[:-1], bounds[1:])))
    got["codes"] = codes

    def make_lists(names):
        for name in names:
            lo, hi = ranges[name]
            lists[name] = listing(got["codes"][lo:hi])
        for name in names:
            lists[name] = tuple(after(x) for x in lists[name])

    wait("codes")
    make_lists(["core"])
    wait(("X", 0))


    def run(name):
        chunks = [chunk_of(key) for key in calls[name]]
        got["acc"] = accumulate(name, flag[0], *lists[name], left, chunks, got["acc"])

    got["DX", 0] = send(got["X", 0], "core")
    got["F"] = send(got["W"], "wrap_cross")
    got["B", 0] = send(got["X", 0], "inner_beside")
    got["X", 1] = send(got["x1"], "pair")
    got["Z", 0] = send(got["X", 0], "along")
    run("core")
    make_lists(["first", "second", "last"])
    wait("acc", ("Z", 0), ("X", 1), ("B", 0), "F", ("DX", 0))
    got["DZ", 0] = send(got["Z", 0], "core")
    got["V"] = send(got["A", None], "wrap_pair")
    got["Z", 1] = send(got["X", 1], "along")
    got["B", 1] = send(got["X", 1], "inner_beside")
    got["C", 0] = send(got["Z", 0], "inner_beside")
    run("first")
    wait("acc", ("C", 0), ("B", 1), ("Z", 1), "V", ("DZ", 0), "ids")
    got["DX", 1] = send(got["X", 1], "core")
    got["DZ", 1] = send(got["Z", 1], "core")
    got["C", 1] = send(got["Z", 1], "inner_beside")
    run("second")
    wait("acc", ("C", 1), ("DZ", 1), ("DX", 1))
    outgoing = finish(
        "last", flag[0], *lists["last"], left, [chunk_of(key) for key in calls["last"]], got["acc"], got["inverse"]
    )
    arrived_ids = got["ids"].reshape(devices * capacity)
    outgoing, arrived_ids = lax.optimization_barrier((outgoing, arrived_ids))
    arrived = lax.all_to_all(outgoing.reshape(-1, order), AXES, split_axis=0, concat_axis=0, tiled=True)
    arrived = arrived.reshape(outgoing.shape)
    return arrived, arrived_ids


def solution(mesh):
    in_specs = (P(AXES, None, None, None), P(AXES, None), P(AXES, None))
    out_specs = (P(AXES, None, None), P(AXES))
    return jax.shard_map(shards, mesh=mesh, in_specs=in_specs, out_specs=out_specs, check_vma=False)
```

```python
import jax
import jax.numpy as jnp
from jax import lax
from jax.experimental import pallas as pl
from jax.experimental.pallas import tpu as pltpu
from jax.sharding import PartitionSpec as P

AXES = ("row", "col")
UNROLL = 24


def at_wrap(r, rows):
    half = rows // 2
    return r in (0, half - 1, half, rows - 1)


def permutations(rows, cols):
    def build(target):
        pairs = []
        for r in range(rows):
            for c in range(cols):
                reached = target(r, c)
                if reached is None:
                    continue
                tr, tc = reached
                pairs.append((r * cols + c, (tr % rows) * cols + tc % cols))
        return pairs

    def beside(r):
        return r + 1 if r % 2 else r - 1

    def along(c):
        return c + 2 if c % 2 == 0 else c - 2

    def only(wrapped, target):
        return build(lambda r, c: target(r, c) if at_wrap(r, rows) == wrapped else None)

    def other(c):
        return c - 1 if c % 2 == 0 else c + 1

    def back(c):
        return c - 2 if c % 2 == 0 else c + 2

    return {
        "pair": build(lambda r, c: (r, c ^ 1)),
        "along": build(lambda r, c: (r, along(c))),
        "far": build(lambda r, c: (r, other(c))),
        "core": build(lambda r, c: (r ^ 1, c)),
        "beside": build(lambda r, c: (beside(r), c)),
        "cross": build(lambda r, c: (beside(r), c ^ 1) if at_wrap(r, rows) else (beside(r), c)),
        "inner_beside": only(False, lambda r, c: (beside(r), c)),
        "wrap_pair": only(True, lambda r, c: (r, c ^ 1)),
        "wrap_back": only(True, lambda r, c: (r, back(c))),
        "wrap_cross": only(True, lambda r, c: (beside(r), c ^ 1)),
    }


def add_entries(count_ref, list_ref, left_ref, pool, acc):
    def group(g, _):
        for q in range(UNROLL):
            code = list_ref[g * UNROLL + q]
            slot = code & 127
            block = (code >> 7) & 1023
            acc[slot] += jnp.dot(
                left_ref[code >> 17], pool[block], preferred_element_type=jnp.float32
            )
        return 0

    lax.fori_loop(0, (count_ref[0] + UNROLL - 1) // UNROLL, group, 0)


def load_pool(flag_ref, refs, chunks, pool, sems):
    refs, copies, start = list(refs), [], 0
    for n, chunk in enumerate(chunks):
        size = chunk[-1].shape[0]
        into = pool.at[pl.ds(start, size)]
        if len(chunk) == 1:
            copies.append(pltpu.make_async_copy(refs.pop(0), into, sems.at[n]))
            copies[-1].start()
        else:
            at_cut = pltpu.make_async_copy(refs.pop(0).at[pl.ds(chunk[1], size)], into, sems.at[n])
            elsewhere = pltpu.make_async_copy(refs.pop(0), into, sems.at[n])
            pl.when(flag_ref[0] != 0)(at_cut.start)
            pl.when(flag_ref[0] == 0)(elsewhere.start)
            copies.append(elsewhere)
        start += size
    return copies


def arrays_of(chunks):
    return [one for chunk in chunks for one in chunk if not isinstance(one, int)]


def accumulate(name, flag, count, entries, left, chunks, acc):
    arrays = arrays_of(chunks)
    n, size = len(arrays), sum(chunk[-1].shape[0] for chunk in chunks)
    order = left.shape[-1]
    slots = left.shape[0] + 8
    fresh = acc is None

    def body(*refs):
        flag_ref, count_ref, list_ref, left_hbm = refs[:4]
        out, total, left_ref, pool, sems = refs[-5:]
        fetch_left = pltpu.make_async_copy(left_hbm, left_ref, sems.at[n + 1])
        fetch_left.start()
        copies = load_pool(flag_ref, refs[4 : 4 + n], chunks, pool, sems)
        if fresh:
            total[...] = jnp.zeros(total.shape, total.dtype)
        else:
            fetch = pltpu.make_async_copy(refs[4 + n], total, sems.at[n])
            fetch.start()
            copies.append(fetch)
        for copy in [fetch_left, *copies]:
            copy.wait()
        add_entries(count_ref, list_ref, left_ref, pool, total)
        store = pltpu.make_async_copy(total, out, sems.at[n])
        store.start()
        store.wait()

    smem = pl.BlockSpec(memory_space=pltpu.SMEM)
    anywhere = pl.BlockSpec(memory_space=pl.ANY)
    args = [flag, count, entries, left, *arrays] + ([] if fresh else [acc])
    return pl.pallas_call(
        body,
        out_shape=jax.ShapeDtypeStruct((slots, order, order), jnp.float32),
        in_specs=[smem] * 3 + [anywhere] * (1 + n + (not fresh)),
        out_specs=anywhere,
        scratch_shapes=[
            pltpu.VMEM((slots, order, order), jnp.float32),
            pltpu.VMEM(left.shape, jnp.bfloat16),
            pltpu.VMEM((size, order, order), jnp.bfloat16),
            pltpu.SemaphoreType.DMA((n + 2,)),
        ],
        input_output_aliases={} if fresh else {4 + n: 0},
        compiler_params=pltpu.CompilerParams(vmem_limit_bytes=58 << 20),
        cost_estimate=pl.CostEstimate(flops=8 << 30, bytes_accessed=32 << 20, transcendentals=0),
        name=name,
    )(*args)


def finish(name, flag, count, entries, left, chunks, acc, inverse):
    arrays = arrays_of(chunks)
    n, size = len(arrays), sum(chunk[-1].shape[0] for chunk in chunks)
    order = left.shape[-1]
    slots = inverse.shape[0]
    part = 16

    def body(*refs):
        flag_ref, count_ref, list_ref, inverse_ref, left_hbm = refs[:5]
        acc_ref, out, total, left_ref, pool, stage, sems, out_sems = refs[5 + n :]
        fetch_left = pltpu.make_async_copy(left_hbm, left_ref, sems.at[n + 1])
        fetch_left.start()
        copies = load_pool(flag_ref, refs[5 : 5 + n], chunks, pool, sems)
        fetch = pltpu.make_async_copy(acc_ref, total, sems.at[n])
        fetch.start()
        for copy in [fetch_left, *copies, fetch]:
            copy.wait()
        add_entries(count_ref, list_ref, left_ref, pool, total)

        def piece(p):
            return pltpu.make_async_copy(
                stage.at[pl.ds(p * part, part)], out.at[pl.ds(p * part, part)], out_sems.at[p]
            )

        def fill(p, _):
            for q in range(part):
                s = p * part + q
                t = inverse_ref[s]
                value = total[jnp.maximum(t, 0)]
                stage[s] = jnp.where(t >= 0, value, 0.0).astype(jnp.bfloat16)
            piece(p).start()
            return 0

        lax.fori_loop(0, slots // part, fill, 0)

        def drain(p, _):
            piece(p).wait()
            return 0

        lax.fori_loop(0, slots // part, drain, 0)

    smem = pl.BlockSpec(memory_space=pltpu.SMEM)
    anywhere = pl.BlockSpec(memory_space=pl.ANY)
    return pl.pallas_call(
        body,
        out_shape=jax.ShapeDtypeStruct((slots, order, order), jnp.bfloat16),
        in_specs=[smem] * 4 + [anywhere] * (n + 2),
        out_specs=anywhere,
        scratch_shapes=[
            pltpu.VMEM(acc.shape, jnp.float32),
            pltpu.VMEM(left.shape, jnp.bfloat16),
            pltpu.VMEM((size, order, order), jnp.bfloat16),
            pltpu.VMEM((slots, order, order), jnp.bfloat16),
            pltpu.SemaphoreType.DMA((n + 2,)),
            pltpu.SemaphoreType.DMA((slots // part,)),
        ],
        compiler_params=pltpu.CompilerParams(vmem_limit_bytes=58 << 20),
        cost_estimate=pl.CostEstimate(flops=0, bytes_accessed=1 << 18, transcendentals=0),
        name=name,
    )(flag, count, entries, inverse, left, *arrays, acc)


def copied(x):
    pieces = 16
    size = x.shape[0] // pieces

    def body(x_ref, out, held, in_sems, out_sems):
        def part(p):
            return pl.ds(p * size, size)

        ins = [pltpu.make_async_copy(x_ref.at[part(p)], held.at[part(p)], in_sems.at[p]) for p in range(pieces)]
        outs = [pltpu.make_async_copy(held.at[part(p)], out.at[part(p)], out_sems.at[p]) for p in range(pieces)]
        for copy in ins:
            copy.start()
        for copy, onward in zip(ins, outs):
            copy.wait()
            onward.start()
        for onward in outs:
            onward.wait()

    anywhere = pl.BlockSpec(memory_space=pl.ANY)
    return pl.pallas_call(
        body,
        out_shape=jax.ShapeDtypeStruct(x.shape, x.dtype),
        in_specs=[anywhere],
        out_specs=anywhere,
        scratch_shapes=[
            pltpu.VMEM(x.shape, x.dtype),
            pltpu.SemaphoreType.DMA((pieces,)),
            pltpu.SemaphoreType.DMA((pieces,)),
        ],
        compiler_params=pltpu.CompilerParams(vmem_limit_bytes=20 << 20),
        name="copied",
    )(x)


def shards(blocks, pattern, owner):
    held, stored, order = blocks.shape[:3]
    rows, cols = lax.axis_size("row"), lax.axis_size("col")
    devices = rows * cols
    r, c = lax.axis_index("row"), lax.axis_index("col")
    here = r * cols + c
    perms = permutations(rows, cols)
    half = rows // 2
    wrap = (r == 0) | (r == half - 1) | (r == half) | (r == rows - 1)
    items = held * stored
    left = blocks.reshape(items, order, order)

    flag = [wrap.astype(jnp.int32).reshape(1)]
    got = {}

    def after(x):
        x, flag[0] = lax.optimization_barrier((x, flag[0]))
        return x

    def wait(*keys):
        for key in keys:
            got[key] = after(got[key])

    def send(x, which):
        return lax.ppermute(after(x), AXES, perms[which])

    pair = c ^ 1
    far = jnp.where(c % 2 == 0, c - 1 + cols, c + 1) % cols
    beside = jnp.where(r % 2 == 1, r + 1, r - 1 + rows) % rows
    holders = {
        "O": here,
        "X": r * cols + pair,
        "Z": r * cols + far,
        "DO": (r ^ 1) * cols + c,
        "DX": (r ^ 1) * cols + pair,
        "DZ": (r ^ 1) * cols + far,
        "A": beside * cols + jnp.where(wrap, pair, c),
        "B": beside * cols + jnp.where(wrap, c, pair),
        "C": beside * cols + far,
    }
    numbers = jnp.arange(stored, dtype=jnp.int32)
    own_slots = jnp.arange(items, dtype=jnp.int32).reshape(held, stored)

    def codes_of(patterns, ids, first):
        into = jnp.max(jnp.where(ids[:, None, None] == pattern[None], own_slots[None], -1), axis=-1)
        to = jnp.max(jnp.where(patterns[:, :, None, None] == pattern[None, None], own_slots[None, None], -1), axis=-1)
        into = into[:, None, :]
        block = (first[:, None] + numbers[None, :])[:, :, None]
        code = (into << 17) | (block << 7) | to
        return jnp.where((into >= 0) & (to >= 0), code, -1).reshape(patterns.shape[0], items)

    def listing(codes):
        codes = codes.reshape(-1)
        total = codes.shape[0]
        length = -(-total // UNROLL) * UNROLL
        ok = codes >= 0
        place = jnp.where(ok, jnp.cumsum(ok.astype(jnp.int32)) - 1, -1)
        count = jnp.sum(ok.astype(jnp.int32)).reshape(1)
        order_of = jnp.arange(length, dtype=jnp.int32)
        listed = jnp.sum(jnp.where(place[None, :] == order_of[:, None], codes[None, :], 0), axis=1)
        return count, jnp.where(order_of < count, listed, items)

    cuts = [(0, 3), (3, 5)]
    whole = (0, held)

    def rows_of(key):
        slot, p = key
        lo, hi = whole if p is None else cuts[p]
        return [(slot, k) for k in range(lo, hi)]

    calls = {
        "core": [("DO", None), ("A", None)],
        "first": [("X", 0), ("X", 1), ("Z", 0), ("DX", 0)],
        "second": [("B", 0), ("B", 1), ("Z", 1), ("C", 0), ("DZ", 0)],
        "last": [("C", 1), ("DZ", 1), ("DX", 1)],
    }

    def chunk_of(key):
        slot, p = key
        if slot in ("B", "C"):
            return (got["V" if slot == "B" else "F"], cuts[p][0] * stored, got[key])
        return (got[key],)

    x0 = left[cuts[0][0] * stored : cuts[0][1] * stored]
    got["DO", None] = send(left, "core")
    got["A", None] = send(left, "cross")
    got["X", 0] = send(x0, "pair")
    got["p2"] = send(pattern, "far")
    got["p1"] = send(pattern, "pair")
    wait("p1", "p2", ("DO", None))
    columns = jnp.stack([pattern, got["p1"], got["p2"]])
    got["W"] = send(left, "wrap_back")
    got["p3"] = send(columns, "core")
    got["p4"] = send(columns, "beside")
    got["x1"] = after(left)[cuts[1][0] * stored : cuts[1][1] * stored]
    own_codes = codes_of(after(pattern), here * held + jnp.arange(held), jnp.arange(held) * stored)
    got["own"] = listing(own_codes)
    wait("own")
    got["acc"] = accumulate("own", flag[0], *got["own"], left, [(left,)], None)
    owners = after(owner).reshape(items)
    number = jnp.arange(items, dtype=jnp.int32)
    earlier = (owners[:, None] == owners[None, :]) & (number[None, :] < number[:, None])
    rank = jnp.sum(earlier.astype(jnp.int32), axis=1)
    capacity = max(2, items // devices + 1)
    target = owners * capacity + rank
    landed = target[None, :] == jnp.arange(devices * capacity, dtype=jnp.int32)[:, None]
    got["inverse"] = jnp.sum(jnp.where(landed, number[None, :] + 1, 0), axis=1) - 1
    outgoing_ids = jnp.where(got["inverse"] >= 0, here * items + got["inverse"], -1)
    got["ids"] = lax.all_to_all(
        after(outgoing_ids).reshape(devices, capacity), AXES, split_axis=0, concat_axis=0, tiled=True
    )
    wait("acc", "W", ("A", None), "x1", "inverse", "p3", "p4")
    lists = {}
    core, near = got["p3"], got["p4"]
    patterns = {
        "O": pattern,
        "X": got["p1"],
        "Z": got["p2"],
        "DO": core[0],
        "DX": core[1],
        "DZ": core[2],
        "A": jnp.where(wrap, near[1], near[0]),
        "B": jnp.where(wrap, near[0], near[1]),
        "C": near[2],
    }
    pats, ids, first, bounds = [], [], [], [0]
    for names in calls.values():
        block = 0
        for key in names:
            for s, k in rows_of(key):
                pats.append(patterns[s][k : k + 1])
                ids.append(holders[s] * held + k)
                first.append(block)
                block += stored
        bounds.append(len(first))
    codes = codes_of(after(jnp.concatenate(pats)), jnp.stack(ids), jnp.asarray(first, jnp.int32))
    ranges = dict(zip(calls, zip(bounds[:-1], bounds[1:])))
    got["codes"] = codes

    def make_lists(names):
        for name in names:
            lo, hi = ranges[name]
            lists[name] = listing(got["codes"][lo:hi])
        for name in names:
            lists[name] = tuple(after(x) for x in lists[name])

    wait("codes")
    make_lists(["core"])
    wait("ids", ("X", 0))


    def run(name):
        chunks = [chunk_of(key) for key in calls[name]]
        got["acc"] = accumulate(name, flag[0], *lists[name], left, chunks, got["acc"])

    got["DX", 0] = send(got["X", 0], "core")
    got["F"] = send(got["W"], "wrap_cross")
    got["B", 0] = send(got["X", 0], "inner_beside")
    got["X", 1] = send(got["x1"], "pair")
    got["Z", 0] = send(got["X", 0], "along")
    run("core")
    make_lists(["first", "second", "last"])
    wait("acc", ("Z", 0), ("X", 1), ("B", 0), "F", ("DX", 0))
    got["DZ", 0] = send(got["Z", 0], "core")
    got["V"] = send(got["A", None], "wrap_pair")
    got["Z", 1] = send(got["X", 1], "along")
    got["B", 1] = send(got["X", 1], "inner_beside")
    got["C", 0] = send(got["Z", 0], "inner_beside")
    run("first")
    wait("acc", ("C", 0), ("B", 1), ("Z", 1), "V", ("DZ", 0))
    got["DX", 1] = send(got["X", 1], "core")
    got["DZ", 1] = send(got["Z", 1], "core")
    got["C", 1] = send(got["Z", 1], "inner_beside")
    run("second")
    wait("acc", ("C", 1), ("DZ", 1), ("DX", 1))
    outgoing = finish(
        "last", flag[0], *lists["last"], left, [chunk_of(key) for key in calls["last"]], got["acc"], got["inverse"]
    )
    arrived_ids = got["ids"].reshape(devices * capacity)
    outgoing, arrived_ids = lax.optimization_barrier((outgoing, arrived_ids))
    arrived = lax.all_to_all(outgoing.reshape(-1, order), AXES, split_axis=0, concat_axis=0, tiled=True)
    arrived = copied(arrived.reshape(outgoing.shape))
    return arrived, arrived_ids


def solution(mesh):
    in_specs = (P(AXES, None, None, None), P(AXES, None), P(AXES, None))
    out_specs = (P(AXES, None, None), P(AXES))
    return jax.shard_map(shards, mesh=mesh, in_specs=in_specs, out_specs=out_specs, check_vma=False)
```

```python
import jax
import jax.numpy as jnp
from jax import lax
from jax.experimental import pallas as pl
from jax.experimental.pallas import tpu as pltpu
from jax.sharding import PartitionSpec as P

AXES = ("row", "col")
UNROLL = 32


def at_wrap(r, rows):
    half = rows // 2
    return r in (0, half - 1, half, rows - 1)


def permutations(rows, cols):
    def build(target):
        pairs = []
        for r in range(rows):
            for c in range(cols):
                reached = target(r, c)
                if reached is None:
                    continue
                tr, tc = reached
                pairs.append((r * cols + c, (tr % rows) * cols + tc % cols))
        return pairs

    def beside(r):
        return r + 1 if r % 2 else r - 1

    def along(c):
        return c + 2 if c % 2 == 0 else c - 2

    def only(wrapped, target):
        return build(lambda r, c: target(r, c) if at_wrap(r, rows) == wrapped else None)

    def other(c):
        return c - 1 if c % 2 == 0 else c + 1

    def back(c):
        return c - 2 if c % 2 == 0 else c + 2

    return {
        "pair": build(lambda r, c: (r, c ^ 1)),
        "along": build(lambda r, c: (r, along(c))),
        "far": build(lambda r, c: (r, other(c))),
        "core": build(lambda r, c: (r ^ 1, c)),
        "beside": build(lambda r, c: (beside(r), c)),
        "cross": build(lambda r, c: (beside(r), c ^ 1) if at_wrap(r, rows) else (beside(r), c)),
        "inner_beside": only(False, lambda r, c: (beside(r), c)),
        "wrap_pair": only(True, lambda r, c: (r, c ^ 1)),
        "wrap_back": only(True, lambda r, c: (r, back(c))),
        "wrap_cross": only(True, lambda r, c: (beside(r), c ^ 1)),
    }


def add_entries(count_ref, list_ref, left_ref, pool, acc):
    def group(g, _):
        for q in range(UNROLL):
            code = list_ref[g * UNROLL + q]
            slot = code & 127
            block = (code >> 7) & 1023
            acc[slot] += jnp.dot(
                left_ref[code >> 17], pool[block], preferred_element_type=jnp.float32
            )
        return 0

    lax.fori_loop(0, (count_ref[0] + UNROLL - 1) // UNROLL, group, 0)


def load_pool(flag_ref, refs, chunks, pool, sems):
    refs, copies, start = list(refs), [], 0
    for n, chunk in enumerate(chunks):
        size = chunk[-1].shape[0]
        into = pool.at[pl.ds(start, size)]
        if len(chunk) == 1:
            copies.append(pltpu.make_async_copy(refs.pop(0), into, sems.at[n]))
            copies[-1].start()
        else:
            at_cut = pltpu.make_async_copy(refs.pop(0).at[pl.ds(chunk[1], size)], into, sems.at[n])
            elsewhere = pltpu.make_async_copy(refs.pop(0), into, sems.at[n])
            pl.when(flag_ref[0] != 0)(at_cut.start)
            pl.when(flag_ref[0] == 0)(elsewhere.start)
            copies.append(elsewhere)
        start += size
    return copies


def arrays_of(chunks):
    return [one for chunk in chunks for one in chunk if not isinstance(one, int)]


def accumulate(name, flag, count, entries, left, chunks, acc):
    arrays = arrays_of(chunks)
    n, size = len(arrays), sum(chunk[-1].shape[0] for chunk in chunks)
    order = left.shape[-1]
    slots = left.shape[0] + 8
    fresh = acc is None

    def body(*refs):
        flag_ref, count_ref, list_ref, left_hbm = refs[:4]
        out, total, left_ref, pool, sems = refs[-5:]
        fetch_left = pltpu.make_async_copy(left_hbm, left_ref, sems.at[n + 1])
        fetch_left.start()
        copies = load_pool(flag_ref, refs[4 : 4 + n], chunks, pool, sems)
        if fresh:
            total[...] = jnp.zeros(total.shape, total.dtype)
        else:
            fetch = pltpu.make_async_copy(refs[4 + n], total, sems.at[n])
            fetch.start()
            copies.append(fetch)
        for copy in [fetch_left, *copies]:
            copy.wait()
        add_entries(count_ref, list_ref, left_ref, pool, total)
        store = pltpu.make_async_copy(total, out, sems.at[n])
        store.start()
        store.wait()

    smem = pl.BlockSpec(memory_space=pltpu.SMEM)
    anywhere = pl.BlockSpec(memory_space=pl.ANY)
    args = [flag, count, entries, left, *arrays] + ([] if fresh else [acc])
    return pl.pallas_call(
        body,
        out_shape=jax.ShapeDtypeStruct((slots, order, order), jnp.float32),
        in_specs=[smem] * 3 + [anywhere] * (1 + n + (not fresh)),
        out_specs=anywhere,
        scratch_shapes=[
            pltpu.VMEM((slots, order, order), jnp.float32),
            pltpu.VMEM(left.shape, jnp.bfloat16),
            pltpu.VMEM((size, order, order), jnp.bfloat16),
            pltpu.SemaphoreType.DMA((n + 2,)),
        ],
        input_output_aliases={} if fresh else {4 + n: 0},
        compiler_params=pltpu.CompilerParams(vmem_limit_bytes=58 << 20),
        cost_estimate=pl.CostEstimate(flops=8 << 30, bytes_accessed=32 << 20, transcendentals=0),
        name=name,
    )(*args)


def finish(name, flag, count, entries, left, chunks, acc, inverse):
    arrays = arrays_of(chunks)
    n, size = len(arrays), sum(chunk[-1].shape[0] for chunk in chunks)
    order = left.shape[-1]
    slots = inverse.shape[0]
    part = 16

    def body(*refs):
        flag_ref, count_ref, list_ref, inverse_ref, left_hbm = refs[:5]
        acc_ref, out, total, left_ref, pool, stage, sems, out_sems = refs[5 + n :]
        fetch_left = pltpu.make_async_copy(left_hbm, left_ref, sems.at[n + 1])
        fetch_left.start()
        copies = load_pool(flag_ref, refs[5 : 5 + n], chunks, pool, sems)
        fetch = pltpu.make_async_copy(acc_ref, total, sems.at[n])
        fetch.start()
        for copy in [fetch_left, *copies, fetch]:
            copy.wait()
        add_entries(count_ref, list_ref, left_ref, pool, total)

        def piece(p):
            return pltpu.make_async_copy(
                stage.at[pl.ds(p * part, part)], out.at[pl.ds(p * part, part)], out_sems.at[p]
            )

        def fill(p, _):
            for q in range(part):
                s = p * part + q
                t = inverse_ref[s]
                value = total[jnp.maximum(t, 0)]
                stage[s] = jnp.where(t >= 0, value, 0.0).astype(jnp.bfloat16)
            piece(p).start()
            return 0

        lax.fori_loop(0, slots // part, fill, 0)

        def drain(p, _):
            piece(p).wait()
            return 0

        lax.fori_loop(0, slots // part, drain, 0)

    smem = pl.BlockSpec(memory_space=pltpu.SMEM)
    anywhere = pl.BlockSpec(memory_space=pl.ANY)
    return pl.pallas_call(
        body,
        out_shape=jax.ShapeDtypeStruct((slots, order, order), jnp.bfloat16),
        in_specs=[smem] * 4 + [anywhere] * (n + 2),
        out_specs=anywhere,
        scratch_shapes=[
            pltpu.VMEM(acc.shape, jnp.float32),
            pltpu.VMEM(left.shape, jnp.bfloat16),
            pltpu.VMEM((size, order, order), jnp.bfloat16),
            pltpu.VMEM((slots, order, order), jnp.bfloat16),
            pltpu.SemaphoreType.DMA((n + 2,)),
            pltpu.SemaphoreType.DMA((slots // part,)),
        ],
        compiler_params=pltpu.CompilerParams(vmem_limit_bytes=58 << 20),
        cost_estimate=pl.CostEstimate(flops=0, bytes_accessed=1 << 18, transcendentals=0),
        name=name,
    )(flag, count, entries, inverse, left, *arrays, acc)


def copied(x):
    pieces = 16
    size = x.shape[0] // pieces

    def body(x_ref, out, held, in_sems, out_sems):
        def part(p):
            return pl.ds(p * size, size)

        ins = [pltpu.make_async_copy(x_ref.at[part(p)], held.at[part(p)], in_sems.at[p]) for p in range(pieces)]
        outs = [pltpu.make_async_copy(held.at[part(p)], out.at[part(p)], out_sems.at[p]) for p in range(pieces)]
        for copy in ins:
            copy.start()
        for copy, onward in zip(ins, outs):
            copy.wait()
            onward.start()
        for onward in outs:
            onward.wait()

    anywhere = pl.BlockSpec(memory_space=pl.ANY)
    return pl.pallas_call(
        body,
        out_shape=jax.ShapeDtypeStruct(x.shape, x.dtype),
        in_specs=[anywhere],
        out_specs=anywhere,
        scratch_shapes=[
            pltpu.VMEM(x.shape, x.dtype),
            pltpu.SemaphoreType.DMA((pieces,)),
            pltpu.SemaphoreType.DMA((pieces,)),
        ],
        compiler_params=pltpu.CompilerParams(vmem_limit_bytes=20 << 20),
        name="copied",
    )(x)


def shards(blocks, pattern, owner):
    held, stored, order = blocks.shape[:3]
    rows, cols = lax.axis_size("row"), lax.axis_size("col")
    devices = rows * cols
    r, c = lax.axis_index("row"), lax.axis_index("col")
    here = r * cols + c
    perms = permutations(rows, cols)
    half = rows // 2
    wrap = (r == 0) | (r == half - 1) | (r == half) | (r == rows - 1)
    items = held * stored
    left = blocks.reshape(items, order, order)

    flag = [wrap.astype(jnp.int32).reshape(1)]
    got = {}

    def after(x):
        x, flag[0] = lax.optimization_barrier((x, flag[0]))
        return x

    def wait(*keys):
        for key in keys:
            got[key] = after(got[key])

    def send(x, which):
        return lax.ppermute(after(x), AXES, perms[which])

    pair = c ^ 1
    far = jnp.where(c % 2 == 0, c - 1 + cols, c + 1) % cols
    beside = jnp.where(r % 2 == 1, r + 1, r - 1 + rows) % rows
    holders = {
        "O": here,
        "X": r * cols + pair,
        "Z": r * cols + far,
        "DO": (r ^ 1) * cols + c,
        "DX": (r ^ 1) * cols + pair,
        "DZ": (r ^ 1) * cols + far,
        "A": beside * cols + jnp.where(wrap, pair, c),
        "B": beside * cols + jnp.where(wrap, c, pair),
        "C": beside * cols + far,
    }
    numbers = jnp.arange(stored, dtype=jnp.int32)
    own_slots = jnp.arange(items, dtype=jnp.int32).reshape(held, stored)

    def codes_of(patterns, ids, first):
        into = jnp.max(jnp.where(ids[:, None, None] == pattern[None], own_slots[None], -1), axis=-1)
        to = jnp.max(jnp.where(patterns[:, :, None, None] == pattern[None, None], own_slots[None, None], -1), axis=-1)
        into = into[:, None, :]
        block = (first[:, None] + numbers[None, :])[:, :, None]
        code = (into << 17) | (block << 7) | to
        return jnp.where((into >= 0) & (to >= 0), code, -1).reshape(patterns.shape[0], items)

    def listing(codes):
        codes = codes.reshape(-1)
        total = codes.shape[0]
        length = -(-total // UNROLL) * UNROLL
        ok = codes >= 0
        place = jnp.where(ok, jnp.cumsum(ok.astype(jnp.int32)) - 1, -1)
        count = jnp.sum(ok.astype(jnp.int32)).reshape(1)
        order_of = jnp.arange(length, dtype=jnp.int32)
        listed = jnp.sum(jnp.where(place[None, :] == order_of[:, None], codes[None, :], 0), axis=1)
        return count, jnp.where(order_of < count, listed, items)

    cuts = [(0, 3), (3, 5)]
    whole = (0, held)

    def rows_of(key):
        slot, p = key
        lo, hi = whole if p is None else cuts[p]
        return [(slot, k) for k in range(lo, hi)]

    calls = {
        "core": [("DO", None), ("A", None)],
        "first": [("X", 0), ("X", 1), ("Z", 0), ("DX", 0)],
        "second": [("B", 0), ("B", 1), ("Z", 1), ("C", 0), ("DZ", 0)],
        "last": [("C", 1), ("DZ", 1), ("DX", 1)],
    }

    def chunk_of(key):
        slot, p = key
        if slot in ("B", "C"):
            return (got["V" if slot == "B" else "F"], cuts[p][0] * stored, got[key])
        return (got[key],)

    x0 = left[cuts[0][0] * stored : cuts[0][1] * stored]
    got["DO", None] = send(left, "core")
    got["A", None] = send(left, "cross")
    got["X", 0] = send(x0, "pair")
    got["p2"] = send(pattern, "far")
    got["p1"] = send(pattern, "pair")
    wait("p1", "p2", ("DO", None))
    columns = jnp.stack([pattern, got["p1"], got["p2"]])
    got["W"] = send(left, "wrap_back")
    got["p3"] = send(columns, "core")
    got["p4"] = send(columns, "beside")
    got["x1"] = after(left)[cuts[1][0] * stored : cuts[1][1] * stored]
    own_codes = codes_of(after(pattern), here * held + jnp.arange(held), jnp.arange(held) * stored)
    got["own"] = listing(own_codes)
    wait("own")
    got["acc"] = accumulate("own", flag[0], *got["own"], left, [(left,)], None)
    owners = after(owner).reshape(items)
    number = jnp.arange(items, dtype=jnp.int32)
    earlier = (owners[:, None] == owners[None, :]) & (number[None, :] < number[:, None])
    rank = jnp.sum(earlier.astype(jnp.int32), axis=1)
    capacity = max(2, items // devices + 1)
    target = owners * capacity + rank
    landed = target[None, :] == jnp.arange(devices * capacity, dtype=jnp.int32)[:, None]
    got["inverse"] = jnp.sum(jnp.where(landed, number[None, :] + 1, 0), axis=1) - 1
    outgoing_ids = jnp.where(got["inverse"] >= 0, here * items + got["inverse"], -1)
    got["ids"] = lax.all_to_all(
        after(outgoing_ids).reshape(devices, capacity), AXES, split_axis=0, concat_axis=0, tiled=True
    )
    wait("acc", "W", ("A", None), "x1", "inverse", "p3", "p4")
    lists = {}
    core, near = got["p3"], got["p4"]
    patterns = {
        "O": pattern,
        "X": got["p1"],
        "Z": got["p2"],
        "DO": core[0],
        "DX": core[1],
        "DZ": core[2],
        "A": jnp.where(wrap, near[1], near[0]),
        "B": jnp.where(wrap, near[0], near[1]),
        "C": near[2],
    }
    pats, ids, first, bounds = [], [], [], [0]
    for names in calls.values():
        block = 0
        for key in names:
            for s, k in rows_of(key):
                pats.append(patterns[s][k : k + 1])
                ids.append(holders[s] * held + k)
                first.append(block)
                block += stored
        bounds.append(len(first))
    codes = codes_of(after(jnp.concatenate(pats)), jnp.stack(ids), jnp.asarray(first, jnp.int32))
    ranges = dict(zip(calls, zip(bounds[:-1], bounds[1:])))
    got["codes"] = codes

    def make_lists(names):
        for name in names:
            lo, hi = ranges[name]
            lists[name] = listing(got["codes"][lo:hi])
        for name in names:
            lists[name] = tuple(after(x) for x in lists[name])

    wait("codes")
    make_lists(["core"])
    wait("ids", ("X", 0))


    def run(name):
        chunks = [chunk_of(key) for key in calls[name]]
        got["acc"] = accumulate(name, flag[0], *lists[name], left, chunks, got["acc"])

    got["DX", 0] = send(got["X", 0], "core")
    got["F"] = send(got["W"], "wrap_cross")
    got["B", 0] = send(got["X", 0], "inner_beside")
    got["X", 1] = send(got["x1"], "pair")
    got["Z", 0] = send(got["X", 0], "along")
    run("core")
    make_lists(["first", "second", "last"])
    wait("acc", ("Z", 0), ("X", 1), ("B", 0), "F", ("DX", 0))
    got["DZ", 0] = send(got["Z", 0], "core")
    got["V"] = send(got["A", None], "wrap_pair")
    got["Z", 1] = send(got["X", 1], "along")
    got["B", 1] = send(got["X", 1], "inner_beside")
    got["C", 0] = send(got["Z", 0], "inner_beside")
    run("first")
    wait("acc", ("C", 0), ("B", 1), ("Z", 1), "V", ("DZ", 0))
    got["DX", 1] = send(got["X", 1], "core")
    got["DZ", 1] = send(got["Z", 1], "core")
    got["C", 1] = send(got["Z", 1], "inner_beside")
    run("second")
    wait("acc", ("C", 1), ("DZ", 1), ("DX", 1))
    outgoing = finish(
        "last", flag[0], *lists["last"], left, [chunk_of(key) for key in calls["last"]], got["acc"], got["inverse"]
    )
    arrived_ids = got["ids"].reshape(devices * capacity)
    outgoing, arrived_ids = lax.optimization_barrier((outgoing, arrived_ids))
    arrived = lax.all_to_all(outgoing.reshape(-1, order), AXES, split_axis=0, concat_axis=0, tiled=True)
    arrived = copied(arrived.reshape(outgoing.shape))
    return arrived, arrived_ids


def solution(mesh):
    in_specs = (P(AXES, None, None, None), P(AXES, None), P(AXES, None))
    out_specs = (P(AXES, None, None), P(AXES))
    return jax.shard_map(shards, mesh=mesh, in_specs=in_specs, out_specs=out_specs, check_vma=False)
```
